512 devices in a mesh: tok: 64 (over x, y, z_lo), pan: 8 (over z_hi, core).
Axes of the slice: x: 4, y: 8, z: 8 (z_hi: 4, z_lo: 2; z = z_hi * 2 + z_lo), core: 2. Of those that a mesh axis runs over, the one named last changes fastest.
Arguments:
- student: bfloat16 [32768, 16384], P('tok', 'pan'), may hold values from -6 to 6
- teacher: bfloat16 [32768, 16384], P('tok', 'pan'), may hold values from -6 to 6
- weight_panel: bfloat16 [16384, 128], P('pan'), may hold values from -6 to 6
Outputs:
- corrected: float32 [16384, 128], P(('pan', 'tok'))
- mismatch: float32 [32768, 128], P('tok')
The draws below stay inside these ranges and needn't reach their ends.
All inputs are finite; a program needn't handle non-finite values.
Results may differ from the reference program's by a relative error of at most 0.0055.
Values may be sent and summed in bfloat16 or wider, within the bound.
No kernel may reach another device: no remote copies, remote signals or barrier semaphores. Data moves between devices by JAX's collectives and lax.ppermute only.
A program may use at most 64 MiB of HBM per device.

```python
import math
import jax
import jax.numpy as jnp
from jax import lax

D = 16384
P_SIZE = 128
ITERS = 2
TOKENS = 32768


def shard_levels(own_key, dims, shards, least, high):
    factor_of = 1.0
    for axis_at, parts in shards:
        heights = jax.random.uniform(jax.random.fold_in(jax.random.fold_in(own_key, 6), axis_at), (parts,), jnp.float32, least / len(shards), high / len(shards))
        factor_of = factor_of * jnp.repeat(jnp.exp(heights), dims[axis_at] // parts).reshape((-1,) + (1,) * (len(dims) - 1 - axis_at))
    return factor_of


def noise(own_key, extent, deviation, bound, pieces=(), dtype=jnp.bfloat16):
    loudness = shard_levels(own_key, extent, pieces, -0.22, 0.18) if pieces else 1.0
    entries = jax.random.normal(own_key, extent, jnp.float32) * deviation * loudness
    return jnp.minimum(jnp.maximum(entries, -bound), bound).astype(dtype)


def setup_inputs(seed: int = 0) -> dict:
    key_of = jax.random.split(jax.random.key(seed), 4)
    student = noise(key_of[0], (TOKENS, D), 1.0, 6.0, ((0, 64), (1, 8)))
    teacher = noise(key_of[1], (TOKENS, D), 1.0, 6.0, ((0, 64), (1, 8)))
    weight_panel = noise(key_of[2], (D, P_SIZE), 1.0, 6.0, ((0, 8),))
    return dict(student=student, teacher=teacher, weight_panel=weight_panel)


def reference(student, teacher, weight_panel):
    scale = 1.0 / math.sqrt(D)
    coef = 0.25 * math.sqrt(D) / TOKENS
    target = jnp.dot(teacher, weight_panel, preferred_element_type=jnp.float32) * scale
    current = weight_panel.astype(jnp.float32)
    mismatch = target - jnp.dot(student, weight_panel, preferred_element_type=jnp.float32) * scale
    for step in range(ITERS):
        rounded = mismatch.astype(jnp.bfloat16)
        gradient = lax.dot_general(student, rounded, (((0,), (0,)), ((), ())), preferred_element_type=jnp.float32)
        current = current + coef * gradient
        panel = current.astype(jnp.bfloat16)
        mismatch = target - jnp.dot(student, panel, preferred_element_type=jnp.float32) * scale
    return (current, mismatch)
```

```python
import math

import jax
import jax.numpy as jnp
from jax import lax
from jax.sharding import PartitionSpec as P

D = 16384
ITERS = 2


def exchange(blocks, axis):
    return lax.all_to_all(blocks, axis, 0, 0, tiled=True)


def spread(own, axis):
    count = lax.axis_size(axis)
    everywhere = jnp.broadcast_to(own[None], (count,) + own.shape)
    got = exchange(everywhere, axis)
    return got.reshape((count * own.shape[0],) + own.shape[1:])


def reduce_rows(partial, axis):
    count = lax.axis_size(axis)
    blocks = partial.astype(jnp.bfloat16).reshape((count, -1) + partial.shape[1:])
    return jnp.sum(exchange(blocks, axis).astype(jnp.float32), axis=0)


def local(student, teacher, weight_panel):
    tok_count = lax.axis_size("tok")
    rows = student.shape[1] // tok_count
    scale = 1.0 / math.sqrt(D)
    coef = 0.25 * math.sqrt(D) / (student.shape[0] * tok_count)
    teacher_part = jnp.dot(teacher, weight_panel, preferred_element_type=jnp.float32)
    student_part = jnp.dot(student, weight_panel, preferred_element_type=jnp.float32)
    mismatch = reduce_rows((teacher_part - student_part) * scale, "pan")
    first_row = lax.axis_index("tok") * rows
    owned = lax.dynamic_slice_in_dim(weight_panel, first_row, rows, 0).astype(jnp.float32)
    for step in range(ITERS):
        rounded = spread(mismatch.astype(jnp.bfloat16), "pan")
        gradient = lax.dot_general(
            student, rounded, (((0,), (0,)), ((), ())), preferred_element_type=jnp.float32
        )
        change = coef * reduce_rows(gradient, "tok")
        owned = owned + change
        moved = jnp.dot(
            student,
            spread(change.astype(jnp.bfloat16), "tok"),
            preferred_element_type=jnp.float32,
        )
        mismatch = mismatch - reduce_rows(moved * scale, "pan")
    return (owned, spread(mismatch, "pan"))


def solution(mesh):
    in_specs = (P("tok", "pan"), P("tok", "pan"), P("pan", None))
    out_specs = (P(("pan", "tok"), None), P("tok", None))
    return jax.shard_map(local, mesh=mesh, in_specs=in_specs, out_specs=out_specs, check_vma=False)
```

```python
import math

import jax
import jax.numpy as jnp
from jax import lax
from jax.sharding import PartitionSpec as P

D = 16384
ITERS = 2
TOK = ("x", "y_hi", "y_lo", "z_lo")
PAN = ("z_hi", "core")
NEAR = ("x", "y_lo", "z_lo")
FAR = ("y_hi",)


def exchange(blocks, axis):
    return lax.all_to_all(blocks, axis, 0, 0, tiled=True)


def copies(own, axis):
    return exchange(jnp.broadcast_to(own[None], (lax.axis_size(axis),) + own.shape), axis)


def add(blocks):
    return jnp.sum(blocks.astype(jnp.float32), axis=0)


def pan_sum(partial):
    rows = partial.shape[0] // lax.axis_size("core")
    both = lax.all_gather(partial, "core", axis=0, tiled=True)
    first_row = lax.axis_index("core") * rows
    here = lax.dynamic_slice_in_dim(both, first_row, rows, 0)
    there = lax.dynamic_slice_in_dim(both, first_row + partial.shape[0], rows, 0)
    return add(copies((here + there).astype(jnp.bfloat16), "z_hi"))


def tok_sum(partial, factor):
    blocks = partial.astype(jnp.bfloat16).reshape((lax.axis_size(NEAR), -1) + partial.shape[1:])
    near = add(exchange(blocks, NEAR)).astype(jnp.bfloat16)
    total = (factor * add(copies(near, FAR))).astype(jnp.bfloat16)
    return copies(total, NEAR).reshape(partial.shape)


def local(student, teacher, weight_panel):
    tok_count = lax.axis_size(TOK)
    rows = student.shape[1] // tok_count
    scale = 1.0 / math.sqrt(D)
    coef = 0.25 * math.sqrt(D) / (student.shape[0] * tok_count)
    first_row = lax.axis_index(TOK) * rows

    def owned_rows(panel):
        return lax.dynamic_slice_in_dim(panel, first_row, rows, 0).astype(jnp.float32)

    teacher_part = jnp.dot(teacher, weight_panel, preferred_element_type=jnp.float32)
    student_part = jnp.dot(student, weight_panel, preferred_element_type=jnp.float32)
    mismatch = pan_sum((teacher_part - student_part) * scale)
    owned = owned_rows(weight_panel)
    for step in range(ITERS):
        rounded = lax.all_gather(mismatch.astype(jnp.bfloat16), "core", axis=0, tiled=True)
        gradient = lax.dot_general(
            student, rounded, (((0,), (0,)), ((), ())), preferred_element_type=jnp.float32
        )
        change = tok_sum(gradient, coef)
        owned = owned + owned_rows(change)
        moved = jnp.dot(student, change, preferred_element_type=jnp.float32)
        mismatch = mismatch - pan_sum(moved * scale)
    return (owned, lax.all_gather(mismatch, "core", axis=0, tiled=True))


def solution(mesh):
    fine = jax.sharding.Mesh(mesh.devices.reshape(4, 4, 2, 2, 4, 2), TOK + PAN)
    in_specs = (P(TOK, PAN), P(TOK, PAN), P(PAN, None))
    out_specs = (P(PAN + TOK, None), P(TOK, None))
    return jax.shard_map(local, mesh=fine, in_specs=in_specs, out_specs=out_specs, check_vma=False)
```

```python
import math

import jax
import jax.numpy as jnp
from jax import lax
from jax.experimental import pallas as pl
from jax.experimental.pallas import tpu as pltpu
from jax.sharding import PartitionSpec as P

D = 16384
ITERS = 2
TOK = ("x", "y_hi", "y_lo", "z_lo")
PAN = ("z_hi", "core")
NEAR = ("x", "y_lo", "z_lo")


def exchange(blocks, axis):
    return lax.all_to_all(blocks, axis, 0, 0, tiled=True)


def copies(own, axis):
    return exchange(jnp.broadcast_to(own[None], (lax.axis_size(axis),) + own.shape), axis)


def add(blocks):
    return jnp.sum(blocks.astype(jnp.float32), axis=0)


def ring_sum(own, axis):
    for pairs in ([[0, 1], [2, 3]], [[1, 2], [3, 0]]):
        both = lax.all_gather(own.astype(jnp.bfloat16), axis, axis=0, tiled=True, axis_index_groups=pairs)
        own = add(both.reshape((2,) + own.shape))
    return own


def hold_kernel(src_ref, out_ref, sem):
    copy = pltpu.make_async_copy(src_ref, out_ref, sem)
    copy.start()
    copy.wait()


def hold(array):
    return pl.pallas_call(
        hold_kernel,
        in_specs=[pl.BlockSpec(memory_space=pl.ANY)],
        out_specs=pl.BlockSpec(memory_space=pltpu.VMEM),
        out_shape=jax.ShapeDtypeStruct(array.shape, array.dtype),
        scratch_shapes=[pltpu.SemaphoreType.DMA],
        compiler_params=pltpu.CompilerParams(vmem_limit_bytes=8 * 1024 * 1024),
        name="hold",
    )(array)


def finish_kernel(core_ref, got_ref, panel_ref, owned_ref, mismatch_ref):
    rows, columns = owned_ref.shape
    tokens = mismatch_ref.shape[0]
    mismatch_ref[...] = got_ref[:, :tokens].T
    last = got_ref[:, tokens:].T
    owned_ref[...] = panel_ref[...] + jnp.where(core_ref[0] == 0, last[:rows], last[rows : 2 * rows])


def finish(core, got, panel_rows, tokens):
    columns = got.shape[0]
    whole = pl.BlockSpec(memory_space=pltpu.VMEM)
    return tuple(
        pl.pallas_call(
            finish_kernel,
            in_specs=[pl.BlockSpec(memory_space=pltpu.SMEM), whole, whole],
            out_specs=[whole, whole],
            out_shape=[
                jax.ShapeDtypeStruct(panel_rows.shape, jnp.float32),
                jax.ShapeDtypeStruct((tokens, columns), jnp.float32),
            ],
            compiler_params=pltpu.CompilerParams(vmem_limit_bytes=8 * 1024 * 1024),
            name="finish",
        )(core, got, panel_rows)
    )


def product(a, b, a_dim, b_dim):
    return lax.dot_general(a, b, (((a_dim,), (b_dim,)), ((), ())), preferred_element_type=jnp.float32)


def split(wide, parts):
    return wide.reshape(wide.shape[0], parts, -1).transpose(1, 0, 2)


def join(blocks):
    return blocks.transpose(1, 0, 2).reshape(blocks.shape[1], -1)


def local(student, teacher, weight_panel):
    tok_count = lax.axis_size(TOK)
    near_count = lax.axis_size(NEAR)
    core = lax.axis_index("core")
    features = student.shape[1]
    tokens = student.shape[0]
    half = weight_panel.shape[1] // 2
    rows = features // tok_count
    scale = 1.0 / math.sqrt(D)
    coef = 0.25 * math.sqrt(D) / (tokens * tok_count)
    first_row = lax.axis_index(TOK) * rows

    student_other = lax.ppermute(student, "core", [(0, 1), (1, 0)])
    student_part = product(weight_panel, student, 0, 1)
    teacher, student_part = lax.optimization_barrier((teacher, student_part))
    partial = (product(weight_panel, teacher, 0, 1) - student_part) * scale
    both = lax.all_gather(partial, "core", axis=0, tiled=True)
    both, student_other = lax.optimization_barrier((both, student_other))
    student_other = hold(student_other)
    here = lax.dynamic_slice_in_dim(both, core * half, half, 0)
    there = lax.dynamic_slice_in_dim(both, core * half + 2 * half, half, 0)
    first, student_other = lax.optimization_barrier(((here + there).astype(jnp.bfloat16), student_other))
    mismatch = add(copies(first, "z_hi"))
    changes = []
    for step in range(ITERS):
        rounded = mismatch.astype(jnp.bfloat16)
        gradient = jnp.concatenate(
            [
                split(product(rounded, part, 1, 0).astype(jnp.bfloat16), near_count // 2)
                for part in (student, student_other)
            ],
            axis=0,
        )
        near = add(exchange(gradient, NEAR))
        change = copies((coef * ring_sum(near, "y_hi")).astype(jnp.bfloat16), NEAR)
        changes.append(change)
        own = join(change[: near_count // 2])
        other = join(change[near_count // 2 :])
        moved = product(own, student, 1, 1) + product(other, student_other, 1, 1)
        if step == ITERS - 1:
            moved, changes, weight_panel = lax.optimization_barrier((moved, changes, weight_panel))
        mismatch = mismatch - add(copies((moved * scale).astype(jnp.bfloat16), "z_hi"))
    width = changes[0].shape[2]
    at = (first_row // width, 0, first_row % width)
    beside = (near_count // 2 + first_row // width, 0, first_row % width)

    def rows_of(start):
        return sum(
            lax.dynamic_slice(change, start, (1, half, rows))[0].astype(jnp.float32) for change in changes
        )

    moved_own, moved_other = rows_of(at), rows_of(beside)
    by_core = jnp.where(
        core == 0,
        jnp.concatenate([moved_own, moved_other], axis=1),
        jnp.concatenate([moved_other, moved_own], axis=1),
    )
    pad = jnp.zeros((half, 128 - 2 * rows), jnp.float32)
    panel_rows = lax.dynamic_slice_in_dim(weight_panel, first_row, rows, 0).astype(jnp.float32)
    got = lax.all_gather(jnp.concatenate([mismatch, by_core, pad], axis=1), "core", axis=0, tiled=True)
    return finish(core.astype(jnp.int32).reshape(1), got, panel_rows, tokens)


def solution(mesh):
    fine = jax.sharding.Mesh(mesh.devices.reshape(4, 4, 2, 2, 4, 2), TOK + PAN)
    in_specs = (P(TOK, PAN), P(TOK, PAN), P(PAN, None))
    out_specs = (P(PAN + TOK, None), P(TOK, None))
    return jax.shard_map(local, mesh=fine, in_specs=in_specs, out_specs=out_specs, check_vma=False)
```

```python
import math

import jax
import jax.numpy as jnp
from jax import lax
from jax.experimental import pallas as pl
from jax.experimental.pallas import tpu as pltpu
from jax.sharding import PartitionSpec as P

D = 16384
ITERS = 2
TOK = ("x", "y_hi", "y_lo", "z_lo")
PAN = ("z_hi", "core")
NEAR = ("x", "y_lo", "z_lo")


def exchange(blocks, axis):
    return lax.all_to_all(blocks, axis, 0, 0, tiled=True)


def copies(own, axis):
    return exchange(jnp.broadcast_to(own[None], (lax.axis_size(axis),) + own.shape), axis)


def add(blocks):
    return jnp.sum(blocks.astype(jnp.float32), axis=0)


def ring_sum(own, axis):
    for pairs in ([[0, 1], [2, 3]], [[1, 2], [3, 0]]):
        both = lax.all_gather(own.astype(jnp.bfloat16), axis, axis=0, tiled=True, axis_index_groups=pairs)
        own = add(both.reshape((2,) + own.shape))
    return own


def hold_kernel(src_ref, out_ref, sem):
    copy = pltpu.make_async_copy(src_ref, out_ref, sem)
    copy.start()
    copy.wait()


def hold(array):
    return pl.pallas_call(
        hold_kernel,
        in_specs=[pl.BlockSpec(memory_space=pl.ANY)],
        out_specs=pl.BlockSpec(memory_space=pltpu.VMEM),
        out_shape=jax.ShapeDtypeStruct(array.shape, array.dtype),
        scratch_shapes=[pltpu.SemaphoreType.DMA],
        compiler_params=pltpu.CompilerParams(vmem_limit_bytes=8 * 1024 * 1024),
        name="hold",
    )(array)


def finish_kernel(core_ref, got_ref, panel_ref, owned_ref, mismatch_ref):
    rows, columns = owned_ref.shape
    tokens = mismatch_ref.shape[0]
    mismatch_ref[...] = got_ref[:, :tokens].T
    last = got_ref[:, tokens:].T
    owned_ref[...] = panel_ref[...] + jnp.where(core_ref[0] == 0, last[:rows], last[rows : 2 * rows])


def finish(core, got, panel_rows, tokens):
    columns = got.shape[0]
    whole = pl.BlockSpec(memory_space=pltpu.VMEM)
    return tuple(
        pl.pallas_call(
            finish_kernel,
            in_specs=[pl.BlockSpec(memory_space=pltpu.SMEM), whole, whole],
            out_specs=[whole, whole],
            out_shape=[
                jax.ShapeDtypeStruct(panel_rows.shape, jnp.float32),
                jax.ShapeDtypeStruct((tokens, columns), jnp.float32),
            ],
            compiler_params=pltpu.CompilerParams(vmem_limit_bytes=8 * 1024 * 1024),
            name="finish",
        )(core, got, panel_rows)
    )


def product(a, b, a_dim, b_dim):
    return lax.dot_general(a, b, (((a_dim,), (b_dim,)), ((), ())), preferred_element_type=jnp.float32)


def split(wide, parts):
    return wide.reshape(wide.shape[0], parts, -1).transpose(1, 0, 2)


def join(blocks):
    return blocks.transpose(1, 0, 2).reshape(blocks.shape[1], -1)


def local(student, teacher, weight_panel):
    tok_count = lax.axis_size(TOK)
    near_count = lax.axis_size(NEAR)
    core = lax.axis_index("core")
    features = student.shape[1]
    tokens = student.shape[0]
    half = weight_panel.shape[1] // 2
    rows = features // tok_count
    scale = 1.0 / math.sqrt(D)
    coef = 0.25 * math.sqrt(D) / (tokens * tok_count)
    first_row = lax.axis_index(TOK) * rows

    student_other = lax.ppermute(student, "core", [(0, 1), (1, 0)])
    student_part = product(weight_panel, student, 0, 1)
    partial = (product(weight_panel, teacher, 0, 1) - student_part) * scale
    both = lax.all_gather(partial, "core", axis=0, tiled=True)
    both, student_other = lax.optimization_barrier((both, student_other))
    student_other = hold(student_other)
    here = lax.dynamic_slice_in_dim(both, core * half, half, 0)
    there = lax.dynamic_slice_in_dim(both, core * half + 2 * half, half, 0)
    first, student_other = lax.optimization_barrier(((here + there).astype(jnp.bfloat16), student_other))
    mismatch = add(copies(first, "z_hi"))
    changes = []
    for step in range(ITERS):
        rounded = mismatch.astype(jnp.bfloat16)
        gradient = jnp.concatenate(
            [
                split(product(rounded, part, 1, 0).astype(jnp.bfloat16), near_count // 2)
                for part in (student, student_other)
            ],
            axis=0,
        )
        near = add(exchange(gradient, NEAR))
        change = copies((coef * ring_sum(near, "y_hi")).astype(jnp.bfloat16), NEAR)
        changes.append(change)
        own = join(change[: near_count // 2])
        other = join(change[near_count // 2 :])
        moved = product(own, student, 1, 1) + product(other, student_other, 1, 1)
        if step == ITERS - 1:
            moved, changes, weight_panel = lax.optimization_barrier((moved, changes, weight_panel))
        mismatch = mismatch - add(copies((moved * scale).astype(jnp.bfloat16), "z_hi"))
    width = changes[0].shape[2]
    at = (first_row // width, 0, first_row % width)
    beside = (near_count // 2 + first_row // width, 0, first_row % width)

    def rows_of(start):
        return sum(
            lax.dynamic_slice(change, start, (1, half, rows))[0].astype(jnp.float32) for change in changes
        )

    moved_own, moved_other = rows_of(at), rows_of(beside)
    by_core = jnp.where(
        core == 0,
        jnp.concatenate([moved_own, moved_other], axis=1),
        jnp.concatenate([moved_other, moved_own], axis=1),
    )
    pad = jnp.zeros((half, 128 - 2 * rows), jnp.float32)
    panel_rows = lax.dynamic_slice_in_dim(weight_panel, first_row, rows, 0).astype(jnp.float32)
    got = lax.all_gather(jnp.concatenate([mismatch, by_core, pad], axis=1), "core", axis=0, tiled=True)
    return finish(core.astype(jnp.int32).reshape(1), got, panel_rows, tokens)


def solution(mesh):
    fine = jax.sharding.Mesh(mesh.devices.reshape(4, 4, 2, 2, 4, 2), TOK + PAN)
    in_specs = (P(TOK, PAN), P(TOK, PAN), P(PAN, None))
    out_specs = (P(PAN + TOK, None), P(TOK, None))
    return jax.shard_map(local, mesh=fine, in_specs=in_specs, out_specs=out_specs, check_vma=False)
```

```python
import math

import jax
import jax.numpy as jnp
from jax import lax
from jax.experimental import pallas as pl
from jax.experimental.pallas import tpu as pltpu
from jax.sharding import PartitionSpec as P

D = 16384
ITERS = 2
TOK = ("x", "y_hi", "y_lo", "z_lo")
PAN = ("z_hi", "core")
NEAR = ("x", "y_lo", "z_lo")


def exchange(blocks, axis):
    return lax.all_to_all(blocks, axis, 0, 0, tiled=True)


def copies(own, axis):
    return exchange(jnp.broadcast_to(own[None], (lax.axis_size(axis),) + own.shape), axis)


def add(blocks):
    return jnp.sum(blocks.astype(jnp.float32), axis=0)


def ring_sum(own, axis):
    for pairs in ([[0, 1], [2, 3]], [[1, 2], [3, 0]]):
        both = lax.all_gather(own.astype(jnp.bfloat16), axis, axis=0, tiled=True, axis_index_groups=pairs)
        own = add(both.reshape((2,) + own.shape))
    return own


def hold_kernel(src_ref, out_ref, sem):
    copy = pltpu.make_async_copy(src_ref, out_ref, sem)
    copy.start()
    copy.wait()


def hold(array):
    return pl.pallas_call(
        hold_kernel,
        in_specs=[pl.BlockSpec(memory_space=pl.ANY)],
        out_specs=pl.BlockSpec(memory_space=pltpu.VMEM),
        out_shape=jax.ShapeDtypeStruct(array.shape, array.dtype),
        scratch_shapes=[pltpu.SemaphoreType.DMA],
        compiler_params=pltpu.CompilerParams(vmem_limit_bytes=8 * 1024 * 1024),
        name="hold",
    )(array)


def finish_kernel(core_ref, got_ref, panel_ref, owned_ref, mismatch_ref):
    rows, columns = owned_ref.shape
    tokens = mismatch_ref.shape[0]
    mismatch_ref[...] = got_ref[:, :tokens].T
    last = got_ref[:, tokens:].T
    owned_ref[...] = panel_ref[...] + jnp.where(core_ref[0] == 0, last[:rows], last[rows : 2 * rows])


def finish(core, got, panel_rows, tokens):
    columns = got.shape[0]
    whole = pl.BlockSpec(memory_space=pltpu.VMEM)
    return tuple(
        pl.pallas_call(
            finish_kernel,
            in_specs=[pl.BlockSpec(memory_space=pltpu.SMEM), whole, whole],
            out_specs=[whole, whole],
            out_shape=[
                jax.ShapeDtypeStruct(panel_rows.shape, jnp.float32),
                jax.ShapeDtypeStruct((tokens, columns), jnp.float32),
            ],
            compiler_params=pltpu.CompilerParams(vmem_limit_bytes=8 * 1024 * 1024),
            name="finish",
        )(core, got, panel_rows)
    )


def join_kernel(got_ref, mismatch_ref, by_core_ref, out_ref):
    tokens = mismatch_ref.shape[1]
    total = got_ref[0].astype(jnp.float32)
    for at in range(1, got_ref.shape[0]):
        total += got_ref[at].astype(jnp.float32)
    out_ref[:, :tokens] = mismatch_ref[...] - total
    out_ref[:, tokens:] = by_core_ref[...]


def last_joined(got, mismatch, by_core):
    whole = pl.BlockSpec(memory_space=pltpu.VMEM)
    shape = (mismatch.shape[0], mismatch.shape[1] + by_core.shape[1])
    return pl.pallas_call(
        join_kernel,
        in_specs=[whole] * 3,
        out_specs=whole,
        out_shape=jax.ShapeDtypeStruct(shape, jnp.float32),
        compiler_params=pltpu.CompilerParams(vmem_limit_bytes=8 * 1024 * 1024),
        name="last_joined",
    )(got, mismatch, by_core)


def product(a, b, a_dim, b_dim):
    return lax.dot_general(a, b, (((a_dim,), (b_dim,)), ((), ())), preferred_element_type=jnp.float32)


def split(wide, parts):
    return wide.reshape(wide.shape[0], parts, -1).transpose(1, 0, 2)


def join(blocks):
    return blocks.transpose(1, 0, 2).reshape(blocks.shape[1], -1)


def local(student, teacher, weight_panel):
    tok_count = lax.axis_size(TOK)
    near_count = lax.axis_size(NEAR)
    core = lax.axis_index("core")
    features = student.shape[1]
    tokens = student.shape[0]
    half = weight_panel.shape[1] // 2
    rows = features // tok_count
    scale = 1.0 / math.sqrt(D)
    coef = 0.25 * math.sqrt(D) / (tokens * tok_count)
    first_row = lax.axis_index(TOK) * rows

    student_other = lax.ppermute(student, "core", [(0, 1), (1, 0)])
    student_part = product(weight_panel, student, 0, 1)
    partial = (product(weight_panel, teacher, 0, 1) - student_part) * scale
    both = lax.all_gather(partial, "core", axis=0, tiled=True)
    both, student_other = lax.optimization_barrier((both, student_other))
    student_other = hold(student_other)
    here = lax.dynamic_slice_in_dim(both, core * half, half, 0)
    there = lax.dynamic_slice_in_dim(both, core * half + 2 * half, half, 0)
    first, student_other = lax.optimization_barrier(((here + there).astype(jnp.bfloat16), student_other))
    mismatch = ring_sum(first, "z_hi")
    changes = []
    for step in range(ITERS):
        rounded = mismatch.astype(jnp.bfloat16)
        gradient = jnp.concatenate(
            [
                split(product(rounded, part, 1, 0).astype(jnp.bfloat16), near_count // 2)
                for part in (student, student_other)
            ],
            axis=0,
        )
        near = add(exchange(gradient, NEAR))
        change = copies((coef * ring_sum(near, "y_hi")).astype(jnp.bfloat16), NEAR)
        changes.append(change)
        own = join(change[: near_count // 2])
        other = join(change[near_count // 2 :])
        moved = product(own, student, 1, 1) + product(other, student_other, 1, 1)
        if step == ITERS - 1:
            moved, changes, weight_panel = lax.optimization_barrier((moved, changes, weight_panel))
        came = copies((moved * scale).astype(jnp.bfloat16), "z_hi")
        if step < ITERS - 1:
            mismatch = mismatch - add(came)
    width = changes[0].shape[2]
    at = (first_row // width, 0, first_row % width)
    beside = (near_count // 2 + first_row // width, 0, first_row % width)

    def rows_of(start):
        return sum(
            lax.dynamic_slice(change, start, (1, half, rows))[0].astype(jnp.float32) for change in changes
        )

    moved_own, moved_other = rows_of(at), rows_of(beside)
    by_core = jnp.where(
        core == 0,
        jnp.concatenate([moved_own, moved_other], axis=1),
        jnp.concatenate([moved_other, moved_own], axis=1),
    )
    pad = jnp.zeros((half, 128 - 2 * rows), jnp.float32)
    panel_rows = lax.dynamic_slice_in_dim(weight_panel, first_row, rows, 0).astype(jnp.float32)
    got = lax.all_gather(last_joined(came, mismatch, jnp.concatenate([by_core, pad], axis=1)), "core", axis=0, tiled=True)
    return finish(core.astype(jnp.int32).reshape(1), got, panel_rows, tokens)


def solution(mesh):
    fine = jax.sharding.Mesh(mesh.devices.reshape(4, 4, 2, 2, 4, 2), TOK + PAN)
    in_specs = (P(TOK, PAN), P(TOK, PAN), P(PAN, None))
    out_specs = (P(PAN + TOK, None), P(TOK, None))
    return jax.shard_map(local, mesh=fine, in_specs=in_specs, out_specs=out_specs, check_vma=False)
```

```python
import math

import jax
import jax.numpy as jnp
from jax import lax
from jax.experimental import pallas as pl
from jax.experimental.pallas import tpu as pltpu
from jax.sharding import PartitionSpec as P

D = 16384
ITERS = 2
TOK = ("x", "y_hi", "y_lo", "z_lo")
PAN = ("z_hi", "core")
NEAR = ("x", "y_lo", "z_lo")


def exchange(blocks, axis):
    return lax.all_to_all(blocks, axis, 0, 0, tiled=True)


def copies(own, axis):
    return exchange(jnp.broadcast_to(own[None], (lax.axis_size(axis),) + own.shape), axis)


def add(blocks):
    return jnp.sum(blocks.astype(jnp.float32), axis=0)


def ring_sum(own, axis):
    for pairs in ([[0, 1], [2, 3]], [[1, 2], [3, 0]]):
        both = lax.all_gather(own.astype(jnp.bfloat16), axis, axis=0, tiled=True, axis_index_groups=pairs)
        own = add(both.reshape((2,) + own.shape))
    return own


def hold_kernel(src_ref, out_ref, sem):
    copy = pltpu.make_async_copy(src_ref, out_ref, sem)
    copy.start()
    copy.wait()


def hold(array):
    return pl.pallas_call(
        hold_kernel,
        in_specs=[pl.BlockSpec(memory_space=pl.ANY)],
        out_specs=pl.BlockSpec(memory_space=pltpu.VMEM),
        out_shape=jax.ShapeDtypeStruct(array.shape, array.dtype),
        scratch_shapes=[pltpu.SemaphoreType.DMA],
        compiler_params=pltpu.CompilerParams(vmem_limit_bytes=8 * 1024 * 1024),
        name="hold",
    )(array)


def finish_kernel(core_ref, got_ref, panel_ref, owned_ref, mismatch_ref):
    rows, columns = owned_ref.shape
    tokens = mismatch_ref.shape[0]
    mismatch_ref[...] = got_ref[:, :tokens].T
    last = got_ref[:, tokens:].T
    owned_ref[...] = panel_ref[...] + jnp.where(core_ref[0] == 0, last[:rows], last[rows : 2 * rows])


def finish(core, got, panel_rows, tokens):
    columns = got.shape[0]
    whole = pl.BlockSpec(memory_space=pltpu.VMEM)
    return tuple(
        pl.pallas_call(
            finish_kernel,
            in_specs=[pl.BlockSpec(memory_space=pltpu.SMEM), whole, whole],
            out_specs=[whole, whole],
            out_shape=[
                jax.ShapeDtypeStruct(panel_rows.shape, jnp.float32),
                jax.ShapeDtypeStruct((tokens, columns), jnp.float32),
            ],
            compiler_params=pltpu.CompilerParams(vmem_limit_bytes=8 * 1024 * 1024),
            name="finish",
        )(core, got, panel_rows)
    )


def join_kernel(got_ref, mismatch_ref, by_core_ref, out_ref):
    tokens = mismatch_ref.shape[1]
    total = got_ref[0].astype(jnp.float32)
    for at in range(1, got_ref.shape[0]):
        total += got_ref[at].astype(jnp.float32)
    out_ref[:, :tokens] = mismatch_ref[...] - total
    out_ref[:, tokens:] = by_core_ref[...]


def last_joined(got, mismatch, by_core):
    whole = pl.BlockSpec(memory_space=pltpu.VMEM)
    shape = (mismatch.shape[0], mismatch.shape[1] + by_core.shape[1])
    return pl.pallas_call(
        join_kernel,
        in_specs=[whole] * 3,
        out_specs=whole,
        out_shape=jax.ShapeDtypeStruct(shape, jnp.float32),
        compiler_params=pltpu.CompilerParams(vmem_limit_bytes=8 * 1024 * 1024),
        name="last_joined",
    )(got, mismatch, by_core)


def product(a, b, a_dim, b_dim):
    return lax.dot_general(a, b, (((a_dim,), (b_dim,)), ((), ())), preferred_element_type=jnp.float32)


def split(wide, parts):
    return wide.reshape(wide.shape[0], parts, -1).transpose(1, 0, 2)


def join(blocks):
    return blocks.transpose(1, 0, 2).reshape(blocks.shape[1], -1)


def local(student, teacher, weight_panel):
    tok_count = lax.axis_size(TOK)
    near_count = lax.axis_size(NEAR)
    core = lax.axis_index("core")
    features = student.shape[1]
    tokens = student.shape[0]
    half = weight_panel.shape[1] // 2
    rows = features // tok_count
    scale = 1.0 / math.sqrt(D)
    coef = 0.25 * math.sqrt(D) / (tokens * tok_count)
    first_row = lax.axis_index(TOK) * rows

    student_other = lax.ppermute(student, "core", [(0, 1), (1, 0)])
    student_part = product(weight_panel, student, 0, 1)
    partial = (product(weight_panel, teacher, 0, 1) - student_part) * scale
    both = lax.all_gather(partial, "core", axis=0, tiled=True)
    both, student_other = lax.optimization_barrier((both, student_other))
    student_other = hold(student_other)
    here = lax.dynamic_slice_in_dim(both, core * half, half, 0)
    there = lax.dynamic_slice_in_dim(both, core * half + 2 * half, half, 0)
    first, student_other = lax.optimization_barrier(((here + there).astype(jnp.bfloat16), student_other))
    mismatch = add(copies(first, "z_hi"))
    changes = []
    for step in range(ITERS):
        rounded = mismatch.astype(jnp.bfloat16)
        gradient = jnp.concatenate(
            [
                split(product(rounded, part, 1, 0).astype(jnp.bfloat16), near_count // 2)
                for part in (student, student_other)
            ],
            axis=0,
        )
        near = add(exchange(gradient, NEAR))
        change = copies((coef * ring_sum(near, "y_hi")).astype(jnp.bfloat16), NEAR)
        changes.append(change)
        own = join(change[: near_count // 2])
        other = join(change[near_count // 2 :])
        moved = product(own, student, 1, 1) + product(other, student_other, 1, 1)
        if step == ITERS - 1:
            moved, changes, weight_panel = lax.optimization_barrier((moved, changes, weight_panel))
        came = copies((moved * scale).astype(jnp.bfloat16), "z_hi")
        if step < ITERS - 1:
            mismatch = mismatch - add(came)
    width = changes[0].shape[2]
    at = (first_row // width, 0, first_row % width)
    beside = (near_count // 2 + first_row // width, 0, first_row % width)

    def rows_of(start):
        return sum(
            lax.dynamic_slice(change, start, (1, half, rows))[0].astype(jnp.float32) for change in changes
        )

    moved_own, moved_other = rows_of(at), rows_of(beside)
    by_core = jnp.where(
        core == 0,
        jnp.concatenate([moved_own, moved_other], axis=1),
        jnp.concatenate([moved_other, moved_own], axis=1),
    )
    pad = jnp.zeros((half, 128 - 2 * rows), jnp.float32)
    panel_rows = lax.dynamic_slice_in_dim(weight_panel, first_row, rows, 0).astype(jnp.float32)
    got = lax.all_gather(last_joined(came, mismatch, jnp.concatenate([by_core, pad], axis=1)), "core", axis=0, tiled=True)
    return finish(core.astype(jnp.int32).reshape(1), got, panel_rows, tokens)


def solution(mesh):
    fine = jax.sharding.Mesh(mesh.devices.reshape(4, 4, 2, 2, 4, 2), TOK + PAN)
    in_specs = (P(TOK, PAN), P(TOK, PAN), P(PAN, None))
    out_specs = (P(PAN + TOK, None), P(TOK, None))
    return jax.shard_map(local, mesh=fine, in_specs=in_specs, out_specs=out_specs, check_vma=False)
```
